512 devices in a mesh: dp: 64 (over z, y), tensor: 8 (over x, core).
Axes of the slice: x: 4, y: 8, z: 8, core: 2. Of those that a mesh axis runs over, the one named last changes fastest.
Arguments:
- tokens: bfloat16 [32768, 4096], P(('dp', 'tensor')), may hold values from -6 to 6
- repack_plan: int32 [32768], P(('dp', 'tensor')), may hold values from 0 to 32767, as said below
- document_ids: int32 [32768], P(('dp', 'tensor')), may hold values from 0 to 255, never falling along the last dimension, each value on 1 to 512 neighbouring positions
- norm_gain: float32 [4096], replicated, may hold values from 0.1 to 1.9
- w_query: bfloat16 [4096, 4096], P('dp', 'tensor'), may hold values from -0.328125 to 0.328125
- w_key: bfloat16 [4096, 1024], P('dp', 'tensor'), may hold values from -0.328125 to 0.328125
- w_value: bfloat16 [4096, 1024], P('dp', 'tensor'), may hold values from -0.09375 to 0.09375
- w_out: bfloat16 [4096, 4096], P('tensor', 'dp'), may hold values from -0.1875 to 0.1875
Outputs:
- attended_out: bfloat16 [32768, 4096], P(('dp', 'tensor'))
The draws below stay inside these ranges and needn't reach their ends.
Inputs may be any that keep to these rules, and one draw needn't show every extreme that they name: A permutation of the rows of the packed array. Token r of the device at dp index i and tensor index t goes to the pack repack_plan[r] // 512, within it to the block of tensor index t (so (repack_plan[r] % 512) // 64 == t); every block of 64 rows of a pack receives one token for each of its rows; of the 64 tokens of one device at most 2 go to one pack, and some device sends exactly 2 to some pack.
All inputs are finite; a program needn't handle non-finite values.
Results may differ from the reference program's by a relative error of at most 0.025.
The reference program's roundings to bfloat16 on the way count: a program that leaves them out, or rounds other values in their place, can miss the bound.
Values may be sent and summed in bfloat16 or wider, within the bound.
No kernel may reach another device: no remote copies, remote signals or barrier semaphores. Data moves between devices by JAX's collectives and lax.ppermute only.
A program may use at most 64 MiB of HBM per device.

```python
import math
import jax
import jax.numpy as jnp
import numpy as np
from jax import lax

D = 4096
HEAD_DIM = 128
HEADS = 32
KV_HEADS = 8
ROWS_DEV = 64
TOK_DEV = 512
TOKENS = 32768
MOST = 2
HEADS_DEV = 4
N_DP = 64
N_TENSOR = 8


def draw_repack_plan(key, part):
    key = jax.random.fold_in(key, 11)
    streams = jax.random.split(key, 3)
    pack_count = TOKENS // TOK_DEV
    tensor_count = TOK_DEV // ROWS_DEV
    half_rows = ROWS_DEV // 2
    grouped = half_rows // MOST
    value_table = jax.vmap(lambda stream: jax.random.permutation(stream, pack_count))(jax.random.split(streams[0], tensor_count))
    shift_table = jax.vmap(lambda stream: jax.random.permutation(stream, pack_count))(jax.random.split(streams[1], tensor_count))
    slot_ids = jnp.arange(ROWS_DEV, dtype=jnp.int32)
    picked = jnp.where(slot_ids < half_rows, slot_ids // MOST, grouped + (slot_ids - half_rows) % (pack_count - grouped))
    offsets = value_table[:, picked]
    orders = jax.vmap(lambda stream: jax.random.permutation(stream, ROWS_DEV))(jax.random.split(streams[2], pack_count * tensor_count))
    orders = orders.reshape(pack_count, tensor_count, ROWS_DEV).astype(jnp.int32)
    sources = jnp.arange(pack_count, dtype=jnp.int32)[:, None, None]
    tensor_ids = jnp.arange(tensor_count, dtype=jnp.int32)[None, :, None]
    offset_of = offsets[tensor_ids, orders]
    shift_of = shift_table[tensor_ids, sources]
    target = (shift_of + offset_of) % pack_count
    plan = target * TOK_DEV + tensor_ids * ROWS_DEV + orders
    return plan.reshape(TOKENS).astype(jnp.int32)


def projection_draw(key, columns):
    values = jnp.clip(jax.random.normal(key, (D, columns), jnp.float32), -4.0, 4.0) / math.sqrt(D)
    return values.astype(jnp.bfloat16)


def draw_w_query(key, part):
    key = jax.random.fold_in(key, 5)
    return projection_draw(key, HEADS * HEAD_DIM)


def draw_w_key(key, part):
    key = jax.random.fold_in(key, 6)
    return projection_draw(key, KV_HEADS * HEAD_DIM)


def levels(rng, dims, pieces, low, largest):
    loudness = 1.0
    for position, parts in pieces:
        steps = jax.random.uniform(jax.random.fold_in(jax.random.fold_in(rng, 6), position), (parts,), jnp.float32, low / len(pieces), largest / len(pieces))
        loudness = loudness * jnp.repeat(jnp.exp(steps), dims[position] // parts).reshape((-1,) + (1,) * (len(dims) - 1 - position))
    return loudness


def split_up(number_of, total, most, skew):
    loads = [(1 << 20) // math.isqrt(standing ** skew) + 1 for standing in range(2, number_of + 1)]
    surplus, counts = total - most - (number_of - 1), [1] * (number_of - 1)
    while surplus > 0:
        free = [i for i in range(number_of - 1) if counts[i] < most]
        mass, left = sum([loads[i] for i in free]), surplus
        for i in free:
            extra = min(most - counts[i], max(1, left * loads[i] // mass), surplus)
            counts[i] = counts[i] + extra
            surplus = surplus - extra
    return np.array([most] + counts)


def uneven_parts(key, number_of, total, most, lean):
    if number_of == 2:
        one = jax.random.randint(key, (), max(1, total - most), min(most, total - 1) + 1)
        return jnp.stack([one, total - one])
    sizes = jnp.asarray(split_up(number_of, total, most, lean), jnp.int32)
    twos = (number_of - 1) // 2
    source_of, sink = sizes[1:1 + 2 * twos:2], sizes[2:2 + 2 * twos:2]
    room = jnp.minimum(source_of - 1, most - sink)
    shifted = jax.random.randint(jax.random.fold_in(key, 1), (twos,), 0, 1 << 20) % (room + 1)
    sizes = sizes.at[1:1 + 2 * twos:2].set(source_of - shifted).at[2:2 + 2 * twos:2].set(sink + shifted)
    return sizes[jax.random.permutation(jax.random.fold_in(key, 2), number_of)]


def bell_draw(rng, extent, width, bound, shards=(), held_as=jnp.bfloat16):
    drawn = jax.random.normal(rng, extent, jnp.float32) * width
    if len(shards) > 0:
        drawn = levels(rng, extent, shards, -0.22, 0.18) * drawn
    return jnp.clip(drawn, min=-bound, max=bound).astype(held_as)


def setup_inputs(seed: int = 0) -> dict:
    keys = jax.random.split(jax.random.key(seed), 9)
    tokens = bell_draw(keys[0], (TOKENS, D), 1.0, 6.0, ((0, 512),))
    repack_plan = draw_repack_plan(jax.random.fold_in(keys[8], 71), 0)
    document_ids = jnp.searchsorted(jnp.cumsum(uneven_parts(keys[2], 4 * N_DP, TOKENS, TOK_DEV, 2)), jnp.arange(TOKENS), side="right").astype(jnp.int32)
    norm_gain = jnp.clip(1.0 + 0.18 * jax.random.normal(keys[3], (D,), jnp.float32), 0.1, 1.9)
    w_query = draw_w_query(jax.random.fold_in(keys[8], 71), 0)
    w_key = draw_w_key(jax.random.fold_in(keys[8], 71), 0)
    w_value = bell_draw(keys[6], (D, KV_HEADS * HEAD_DIM), D ** -0.5, 0.09375, ((0, 64), (1, 8)))
    w_out = bell_draw(keys[7], (HEADS * HEAD_DIM, D), (HEADS * HEAD_DIM // 4) ** -0.5, 0.1875, ((0, 8), (1, 64)))
    return {"tokens": tokens, "repack_plan": repack_plan, "document_ids": document_ids, "norm_gain": norm_gain, "w_query": w_query, "w_key": w_key, "w_value": w_value, "w_out": w_out}


def rms_rows(states, norm_gain):
    floats = states.astype(jnp.float32)
    mean_square = lax.optimization_barrier(jnp.mean(floats * floats, axis=-1, keepdims=True))
    return (floats * lax.rsqrt(mean_square + 1e-05) * norm_gain.astype(jnp.float32)).astype(jnp.bfloat16)

def attend_pack(query, key_rows, value_rows, doc_rows):
    count = query.shape[0]
    kv_count = key_rows.shape[1] // HEAD_DIM
    group = query.shape[1] // HEAD_DIM // kv_count
    queries = query.reshape(count, kv_count, group, HEAD_DIM).astype(jnp.float32)
    keys_f = key_rows.reshape(count, kv_count, HEAD_DIM).astype(jnp.float32)
    values_f = value_rows.reshape(count, kv_count, HEAD_DIM).astype(jnp.float32)
    scores = jnp.einsum('thgd,shd->hgts', queries, keys_f) / jnp.sqrt(jnp.float32(HEAD_DIM))
    positions = jnp.arange(count, dtype=jnp.int32)
    allowed = (doc_rows[:, None] == doc_rows[None, :]) & (positions[:, None] >= positions[None, :])
    scores = jnp.where(allowed, scores, jnp.float32(-1e+30))
    highest = lax.optimization_barrier(jnp.max(scores, axis=-1, keepdims=True))
    weights = jnp.where(allowed, jnp.exp(scores - highest), jnp.float32(0.0))
    probs = (weights / lax.optimization_barrier(jnp.sum(weights, axis=-1, keepdims=True))).astype(jnp.bfloat16)
    mixed = jnp.einsum('hgts,shd->thgd', probs.astype(jnp.float32), values_f)
    return mixed.reshape(count, kv_count * group * HEAD_DIM).astype(jnp.bfloat16)

def reference(tokens, repack_plan, document_ids, norm_gain, w_query, w_key, w_value, w_out):
    packed = jnp.zeros_like(tokens).at[repack_plan].set(tokens)
    normed = rms_rows(packed, norm_gain)
    query = jnp.dot(normed, w_query, preferred_element_type=jnp.float32).astype(jnp.bfloat16)
    key_rows = jnp.dot(normed, w_key, preferred_element_type=jnp.float32).astype(jnp.bfloat16)
    value_rows = jnp.dot(normed, w_value, preferred_element_type=jnp.float32).astype(jnp.bfloat16)
    pack_count = TOKENS // TOK_DEV
    stacked = (query.reshape(pack_count, TOK_DEV, -1), key_rows.reshape(pack_count, TOK_DEV, -1), value_rows.reshape(pack_count, TOK_DEV, -1), document_ids.reshape(pack_count, TOK_DEV))
    attended = lax.map(lambda items: attend_pack(items[0], items[1], items[2], items[3]), stacked)
    attended = attended.reshape(TOKENS, HEADS * HEAD_DIM)
    group_width = HEADS_DEV * HEAD_DIM
    total = jnp.zeros((TOKENS, D), jnp.float32)
    for group_index in range(N_TENSOR):
        lower = group_index * group_width
        partial_value = jnp.dot(attended[:, lower:lower + group_width], w_out[lower:lower + group_width], preferred_element_type=jnp.float32)
        rounded = lax.optimization_barrier(partial_value.astype(jnp.bfloat16))
        total = total + rounded.astype(jnp.float32)
    return total.astype(jnp.bfloat16)
```

```python
import jax
import jax.numpy as jnp
from jax import lax
from jax.sharding import Mesh, PartitionSpec as P

HEAD_DIM = 128
LANES = 128


def rms_rows(states, norm_gain):
    floats = states.astype(jnp.float32)
    mean_square = jnp.mean(floats * floats, axis=-1, keepdims=True)
    return (floats * lax.rsqrt(mean_square + 1e-05) * norm_gain).astype(jnp.bfloat16)


def attend_pack(query, key_rows, value_rows, doc_rows, positions):
    count = query.shape[0]
    group = query.shape[1] // HEAD_DIM
    queries = query.reshape(count, group, HEAD_DIM)
    scores = jnp.einsum("tgd,sd->gts", queries, key_rows, preferred_element_type=jnp.float32)
    scores = scores / jnp.sqrt(jnp.float32(HEAD_DIM))
    allowed = (doc_rows[:, None] == doc_rows[None, :]) & (positions[:, None] >= positions[None, :])
    scores = jnp.where(allowed, scores, jnp.float32(-1e30))
    highest = jnp.max(scores, axis=-1, keepdims=True)
    weights = jnp.where(allowed, jnp.exp(scores - highest), jnp.float32(0.0))
    probs = (weights / jnp.sum(weights, axis=-1, keepdims=True)).astype(jnp.bfloat16)
    mixed = jnp.einsum("gts,sd->tgd", probs, value_rows, preferred_element_type=jnp.float32)
    return mixed.reshape(count, group * HEAD_DIM).astype(jnp.bfloat16)


def shift(array, axis, step, size):
    return lax.ppermute(array, axis, [(i, (i + step) % size) for i in range(size)])


def on_device(tokens, repack_plan, document_ids, norm_gain, w_query, w_key, w_value, w_out):
    dp = ("z", "y")
    row_count, width = tokens.shape
    x_count = lax.axis_size("x")
    peer_count = lax.axis_size("z") * lax.axis_size("y")
    x_index = lax.axis_index("x")
    core_index = lax.axis_index("core")
    pack_rows = row_count * x_count * 2
    projection = w_query.shape[1] + w_key.shape[1] + w_value.shape[1]

    with jax.named_scope("weights"):
        own_weights = jnp.concatenate([w_query, w_key, w_value, w_out.T], axis=1)
        weights = lax.all_gather(own_weights, dp, axis=0, tiled=True)

    with jax.named_scope("dispatch"):
        capacity = 2
        slot_count = peer_count * capacity
        target = repack_plan // pack_rows
        landing = repack_plan % row_count
        positions = jnp.arange(row_count, dtype=jnp.int32)
        same_pack = target[:, None] == target[None, :]
        earlier = positions[None, :] < positions[:, None]
        slot_rank = jnp.sum(jnp.where(same_pack & earlier, 1, 0), axis=1).astype(jnp.int32)
        slot_of = target * capacity + slot_rank
        selector = slot_of[None, :] == jnp.arange(slot_count, dtype=jnp.int32)[:, None]
        marks = jnp.broadcast_to((landing + 1)[:, None], (row_count, LANES)).astype(jnp.bfloat16)
        outgoing = jnp.dot(
            selector.astype(jnp.bfloat16),
            jnp.concatenate([tokens, marks], axis=1),
            preferred_element_type=jnp.float32,
        ).astype(jnp.bfloat16)
        arrived = lax.all_to_all(outgoing, dp, split_axis=0, concat_axis=0, tiled=True)
        arrived_marks = arrived[:, width].astype(jnp.int32)
        settle = arrived_marks[None, :] == positions[:, None] + 1
        owned = jnp.dot(
            settle.astype(jnp.bfloat16), arrived[:, :width], preferred_element_type=jnp.float32
        ).astype(jnp.bfloat16)
        normed_own = rms_rows(owned, norm_gain)

    with jax.named_scope("pack_rows"):
        docs = lax.all_gather(document_ids, ("x", "core"), axis=0, tiled=False)
        rings = [normed_own] + [shift(normed_own, "x", -k, x_count) for k in range(1, x_count)]
        near = jnp.concatenate(rings, axis=0)
        far = shift(near, "core", 1, 2)
        normed = jnp.concatenate([near, far], axis=0)
        ring_of = (x_index + jnp.arange(x_count, dtype=jnp.int32)) % x_count
        block_of = jnp.concatenate([ring_of * 2 + core_index, ring_of * 2 + 1 - core_index])
        doc_rows = docs[block_of].reshape(pack_rows)
        pack_positions = (block_of[:, None] * row_count + positions[None, :]).reshape(pack_rows)

    with jax.named_scope("attention"):
        sums = jnp.dot(normed, weights[:, :projection], preferred_element_type=jnp.float32)
        sums = sums.astype(jnp.bfloat16)
        q_end = w_query.shape[1]
        k_end = q_end + w_key.shape[1]
        attended = attend_pack(
            sums[:, :q_end], sums[:, q_end:k_end], sums[:, k_end:], doc_rows, pack_positions
        )

    with jax.named_scope("output"):
        halves = attended.reshape(2, x_count, row_count, -1)
        ordered = jnp.roll(halves, x_index, axis=1).reshape(2, x_count * row_count, -1)
        out_rows = weights[:, projection:]
        dims = (((1,), (1,)), ((), ()))
        theirs = lax.dot_general(ordered[1], out_rows, dims, preferred_element_type=jnp.float32)
        received = shift(theirs.astype(jnp.bfloat16), "core", 1, 2)
        ours = lax.dot_general(ordered[0], out_rows, dims, preferred_element_type=jnp.float32)
        both = (ours + received.astype(jnp.float32)).astype(jnp.bfloat16)
        return lax.psum_scatter(both, "x", scatter_dimension=0, tiled=True)


def solution(mesh):
    grid = Mesh(mesh.devices.reshape(8, 8, 4, 2), ("z", "y", "x", "core"))
    dp, tensor, rows = ("z", "y"), ("x", "core"), ("z", "y", "x", "core")
    return jax.shard_map(
        on_device,
        mesh=grid,
        in_specs=(
            P(rows, None),
            P(rows),
            P(rows),
            P(),
            P(dp, tensor),
            P(dp, tensor),
            P(dp, tensor),
            P(tensor, dp),
        ),
        out_specs=P(rows, None),
        check_vma=False,
    )
```

```python
import jax
import jax.numpy as jnp
from jax import lax
from jax.sharding import Mesh, PartitionSpec as P

HEAD_DIM = 128
LANES = 128


def rms_rows(states, norm_gain):
    floats = states.astype(jnp.float32)
    mean_square = jnp.mean(floats * floats, axis=-1, keepdims=True)
    return (floats * lax.rsqrt(mean_square + 1e-05) * norm_gain).astype(jnp.bfloat16)


def attend_pack(query, key_rows, value_rows, doc_rows, positions):
    count = query.shape[0]
    group = query.shape[1] // HEAD_DIM
    queries = query.reshape(count, group, HEAD_DIM)
    scores = jnp.einsum("tgd,sd->gts", queries, key_rows, preferred_element_type=jnp.float32)
    scores = scores / jnp.sqrt(jnp.float32(HEAD_DIM))
    allowed = (doc_rows[:, None] == doc_rows[None, :]) & (positions[:, None] >= positions[None, :])
    scores = jnp.where(allowed, scores, jnp.float32(-1e30))
    highest = jnp.max(scores, axis=-1, keepdims=True)
    weights = jnp.where(allowed, jnp.exp(scores - highest), jnp.float32(0.0))
    probs = (weights / jnp.sum(weights, axis=-1, keepdims=True)).astype(jnp.bfloat16)
    mixed = jnp.einsum("gts,sd->tgd", probs, value_rows, preferred_element_type=jnp.float32)
    return mixed.reshape(count, group * HEAD_DIM).astype(jnp.bfloat16)


def shift(array, axis, step, size):
    return lax.ppermute(array, axis, [(i, (i + step) % size) for i in range(size)])


def on_device(tokens, repack_plan, document_ids, norm_gain, w_query, w_key, w_value, w_out):
    dp = ("z", "y")
    row_count, width = tokens.shape
    x_count = lax.axis_size("x")
    peer_count = lax.axis_size("z") * lax.axis_size("y")
    core_index = lax.axis_index("core")
    pack_rows = row_count * x_count * 2
    projection = w_query.shape[1] + w_key.shape[1] + w_value.shape[1]

    with jax.named_scope("weights"):
        own_weights = jnp.concatenate([w_query, w_key, w_value, w_out.T], axis=1)
        weights = lax.all_gather(own_weights, dp, axis=0, tiled=True)

    with jax.named_scope("dispatch"):
        capacity = 2
        slot_count = peer_count * capacity
        target = repack_plan // pack_rows
        landing = repack_plan % row_count
        positions = jnp.arange(row_count, dtype=jnp.int32)
        same_pack = target[:, None] == target[None, :]
        earlier = positions[None, :] < positions[:, None]
        slot_rank = jnp.sum(jnp.where(same_pack & earlier, 1, 0), axis=1).astype(jnp.int32)
        slot_of = target * capacity + slot_rank
        selector = slot_of[None, :] == jnp.arange(slot_count, dtype=jnp.int32)[:, None]
        marks = jnp.broadcast_to((landing + 1)[:, None], (row_count, LANES)).astype(jnp.bfloat16)
        outgoing = jnp.dot(
            selector.astype(jnp.bfloat16),
            jnp.concatenate([tokens, marks], axis=1),
            preferred_element_type=jnp.float32,
        ).astype(jnp.bfloat16)
        arrived = lax.all_to_all(outgoing, dp, split_axis=0, concat_axis=0, tiled=True)
        arrived_marks = arrived[:, width].astype(jnp.int32)
        settle = arrived_marks[None, :] == positions[:, None] + 1
        owned = jnp.dot(
            settle.astype(jnp.bfloat16), arrived[:, :width], preferred_element_type=jnp.float32
        ).astype(jnp.bfloat16)
        normed_own = rms_rows(owned, norm_gain)

    with jax.named_scope("pack_rows"):
        docs = lax.all_gather(document_ids, ("x", "core"), axis=0, tiled=False)
        copies = jnp.broadcast_to(normed_own[None], (x_count,) + normed_own.shape)
        near = lax.all_to_all(copies, "x", split_axis=0, concat_axis=0, tiled=True)
        near = near.reshape(x_count * row_count, width)
        far = shift(near, "core", 1, 2)
        normed = jnp.concatenate([near, far], axis=0)
        even = 2 * jnp.arange(x_count, dtype=jnp.int32)
        block_of = jnp.concatenate([even + core_index, even + 1 - core_index])
        doc_rows = docs[block_of].reshape(pack_rows)
        pack_positions = (block_of[:, None] * row_count + positions[None, :]).reshape(pack_rows)

    with jax.named_scope("attention"):
        sums = jnp.dot(normed, weights[:, :projection], preferred_element_type=jnp.float32)
        sums = sums.astype(jnp.bfloat16)
        q_end = w_query.shape[1]
        k_end = q_end + w_key.shape[1]
        attended = attend_pack(
            sums[:, :q_end], sums[:, q_end:k_end], sums[:, k_end:], doc_rows, pack_positions
        )

    with jax.named_scope("output"):
        half = x_count * row_count
        out_rows = weights[:, projection:]
        dims = (((1,), (1,)), ((), ()))
        theirs = lax.dot_general(attended[half:], out_rows, dims, preferred_element_type=jnp.float32)
        received = shift(theirs.astype(jnp.bfloat16), "core", 1, 2)
        ours = lax.dot_general(attended[:half], out_rows, dims, preferred_element_type=jnp.float32)
        ours = lax.optimization_barrier(ours.astype(jnp.bfloat16))
        both = (ours.astype(jnp.float32) + received.astype(jnp.float32)).astype(jnp.bfloat16)
        parts = lax.all_to_all(both, "x", split_axis=0, concat_axis=0, tiled=True)
        parts = parts.reshape(x_count, row_count, -1).astype(jnp.float32)
        return jnp.sum(parts, axis=0).astype(jnp.bfloat16)


def solution(mesh):
    grid = Mesh(mesh.devices.reshape(8, 8, 4, 2), ("z", "y", "x", "core"))
    dp, tensor, rows = ("z", "y"), ("x", "core"), ("z", "y", "x", "core")
    return jax.shard_map(
        on_device,
        mesh=grid,
        in_specs=(
            P(rows, None),
            P(rows),
            P(rows),
            P(),
            P(dp, tensor),
            P(dp, tensor),
            P(dp, tensor),
            P(tensor, dp),
        ),
        out_specs=P(rows, None),
        check_vma=False,
    )
```

```python
import math

import jax
import jax.numpy as jnp
from jax import lax
from jax.experimental import pallas as pl
from jax.experimental.pallas import tpu as pltpu
from jax.sharding import Mesh, PartitionSpec as P

HEAD_DIM = 128
LANES = 128
CHUNK = 512
VMEM_BYTES = 32 * 1024 * 1024


def rms_rows(states, norm_gain):
    floats = states.astype(jnp.float32)
    mean_square = jnp.mean(floats * floats, axis=-1, keepdims=True)
    return (floats * lax.rsqrt(mean_square + 1e-05) * norm_gain).astype(jnp.bfloat16)


def attention_kernel(
    near,
    far,
    weights,
    doc_column,
    doc_row,
    place_column,
    place_row,
    attended,
    total,
    held,
    loaded,
    arrivals,
):
    half, width = near.shape
    projection = loaded.shape[1]
    group = attended.shape[1] // HEAD_DIM
    halves = [slice(0, half), slice(half, 2 * half)]
    chunks = [slice(start, start + CHUNK) for start in range(0, width, CHUNK)]
    copies = [
        pltpu.make_async_copy(
            weights.at[pl.ds(chunk.start, CHUNK), pl.ds(0, projection)],
            loaded.at[pl.ds(chunk.start, CHUNK), :],
            arrivals.at[index],
        )
        for index, chunk in enumerate(chunks)
    ]
    for copy in copies:
        copy.start()
    for copy, chunk in zip(copies, chunks):
        copy.wait()
        for here, rows in zip(halves, (near, far)):
            term = jnp.dot(
                rows[:, chunk], loaded[chunk, :], preferred_element_type=jnp.float32
            )
            if chunk.start == 0:
                total[here, :] = term
            elif chunk.stop < width:
                total[here, :] += term
            else:
                held[here, :] = (total[here, :] + term).astype(jnp.bfloat16)
    key_at = group * HEAD_DIM
    keys = held[:, key_at : key_at + HEAD_DIM]
    values = held[:, key_at + HEAD_DIM : key_at + 2 * HEAD_DIM]
    scale = HEAD_DIM**-0.5 * math.log2(math.e)
    for here in halves:
        same = doc_column[here, :] == doc_row[...]
        allowed = same & (place_column[here, :] >= place_row[...])
        hidden = jnp.where(allowed, 0.0, -1e30)
        for head in range(group):
            lanes = slice(head * HEAD_DIM, (head + 1) * HEAD_DIM)
            scores = lax.dot_general(
                held[here, lanes], keys, (((1,), (1,)), ((), ())), preferred_element_type=jnp.float32
            )
            scores = scores * scale + hidden
            weight = jnp.exp2(scores - jnp.max(scores, axis=1, keepdims=True))
            share = 1.0 / jnp.sum(weight, axis=1, keepdims=True)
            mixed = jnp.dot(weight.astype(jnp.bfloat16), values, preferred_element_type=jnp.float32)
            attended[here, lanes] = (mixed * share).astype(jnp.bfloat16)


def attention(near, far, weights, docs, places, projection, head_columns):
    half, width = near.shape
    rows = 2 * half
    here = pl.BlockSpec(memory_space=pltpu.VMEM)
    return pl.pallas_call(
        attention_kernel,
        out_shape=jax.ShapeDtypeStruct((rows, head_columns), jnp.bfloat16),
        in_specs=[here, here, pl.BlockSpec(memory_space=pl.ANY), here, here, here, here],
        out_specs=here,
        scratch_shapes=[
            pltpu.VMEM((rows, projection), jnp.float32),
            pltpu.VMEM((rows, projection), jnp.bfloat16),
            pltpu.VMEM((width, projection), jnp.bfloat16),
            pltpu.SemaphoreType.DMA((width // CHUNK,)),
        ],
        compiler_params=pltpu.CompilerParams(vmem_limit_bytes=VMEM_BYTES),
        cost_estimate=pl.CostEstimate(
            flops=2 * rows * width * projection + 4 * rows * rows * head_columns,
            bytes_accessed=2 * width * (rows + projection) + 2 * rows * head_columns,
            transcendentals=rows * rows * head_columns // HEAD_DIM,
        ),
        name="attention",
    )(near, far, weights, docs[:, None], docs[None, :], places[:, None], places[None, :])


def shift(array, axis, step, size):
    return lax.ppermute(array, axis, [(i, (i + step) % size) for i in range(size)])


def on_device(tokens, repack_plan, document_ids, norm_gain, w_query, w_key, w_value, w_out):
    dp = ("z", "y")
    row_count, width = tokens.shape
    x_count = lax.axis_size("x")
    peer_count = lax.axis_size("z") * lax.axis_size("y")
    core_index = lax.axis_index("core")
    pack_rows = row_count * x_count * 2
    projection = w_query.shape[1] + w_key.shape[1] + w_value.shape[1]

    with jax.named_scope("weights"):
        own_weights = jnp.concatenate([w_query, w_key, w_value, w_out.T], axis=1)
        weights = lax.all_gather(own_weights, dp, axis=0, tiled=True)

    with jax.named_scope("dispatch"):
        capacity = 2
        slot_count = peer_count * capacity
        target = repack_plan // pack_rows
        landing = repack_plan % row_count
        positions = jnp.arange(row_count, dtype=jnp.int32)
        same_pack = target[:, None] == target[None, :]
        earlier = positions[None, :] < positions[:, None]
        slot_rank = jnp.sum(jnp.where(same_pack & earlier, 1, 0), axis=1).astype(jnp.int32)
        slot_of = target * capacity + slot_rank
        selector = slot_of[None, :] == jnp.arange(slot_count, dtype=jnp.int32)[:, None]
        marks = jnp.broadcast_to((landing + 1)[:, None], (row_count, LANES)).astype(jnp.bfloat16)
        outgoing = jnp.dot(
            selector.astype(jnp.bfloat16),
            jnp.concatenate([tokens, marks], axis=1),
            preferred_element_type=jnp.float32,
        ).astype(jnp.bfloat16)
        arrived = lax.all_to_all(outgoing, dp, split_axis=0, concat_axis=0, tiled=True)
        arrived_marks = arrived[:, width].astype(jnp.int32)
        settle = arrived_marks[None, :] == positions[:, None] + 1
        owned = jnp.dot(
            settle.astype(jnp.bfloat16), arrived[:, :width], preferred_element_type=jnp.float32
        ).astype(jnp.bfloat16)
        normed_own = rms_rows(owned, norm_gain)

    with jax.named_scope("pack_rows"):
        docs = lax.all_gather(document_ids, ("x", "core"), axis=0, tiled=False)
        copies = jnp.broadcast_to(normed_own[None], (x_count,) + normed_own.shape)
        near = lax.all_to_all(copies, "x", split_axis=0, concat_axis=0, tiled=True)
        near = near.reshape(x_count * row_count, width)
        far = shift(near, "core", 1, 2)
        even = 2 * jnp.arange(x_count, dtype=jnp.int32)
        block_of = jnp.concatenate([even + core_index, even + 1 - core_index])
        doc_rows = docs[block_of].reshape(pack_rows)
        pack_positions = (block_of[:, None] * row_count + positions[None, :]).reshape(pack_rows)

    with jax.named_scope("attention"):
        attended = attention(
            near, far, weights, doc_rows, pack_positions, projection, w_query.shape[1]
        )

    with jax.named_scope("output"):
        half = x_count * row_count
        out_rows = weights[:, projection:]
        dims = (((1,), (1,)), ((), ()))
        theirs = lax.dot_general(attended[half:], out_rows, dims, preferred_element_type=jnp.float32)
        received = shift(theirs.astype(jnp.bfloat16), "core", 1, 2)
        ours = lax.dot_general(attended[:half], out_rows, dims, preferred_element_type=jnp.float32)
        ours = lax.optimization_barrier(ours.astype(jnp.bfloat16))
        both = (ours.astype(jnp.float32) + received.astype(jnp.float32)).astype(jnp.bfloat16)
        parts = lax.all_to_all(both, "x", split_axis=0, concat_axis=0, tiled=True)
        parts = parts.reshape(x_count, row_count, -1).astype(jnp.float32)
        return jnp.sum(parts, axis=0).astype(jnp.bfloat16)


def solution(mesh):
    grid = Mesh(mesh.devices.reshape(8, 8, 4, 2), ("z", "y", "x", "core"))
    dp, tensor, rows = ("z", "y"), ("x", "core"), ("z", "y", "x", "core")
    return jax.shard_map(
        on_device,
        mesh=grid,
        in_specs=(
            P(rows, None),
            P(rows),
            P(rows),
            P(),
            P(dp, tensor),
            P(dp, tensor),
            P(dp, tensor),
            P(tensor, dp),
        ),
        out_specs=P(rows, None),
        check_vma=False,
    )
```

```python
import functools
import math

import jax
import jax.numpy as jnp
from jax import lax
from jax.experimental import pallas as pl
from jax.experimental.pallas import tpu as pltpu
from jax.sharding import Mesh, PartitionSpec as P

HEAD_DIM = 128
LANES = 128
SIDE = 8
ROWS = 64
VMEM_BYTES = 16 * 1024 * 1024
PLANE = ("z", "y", "core")


def rms_rows(states, norm_gain):
    floats = states.astype(jnp.float32)
    mean_square = jnp.mean(floats * floats, axis=-1, keepdims=True)
    return (floats * lax.rsqrt(mean_square + 1e-05) * norm_gain).astype(jnp.bfloat16)


def shift(array, axis, step):
    size = lax.axis_size(axis)
    return lax.ppermute(array, axis, [(i, (i + step) % size) for i in range(size)])


def spread(block, axis):
    size = lax.axis_size(axis)
    copies = jnp.broadcast_to(block[None], (size,) + block.shape)
    return lax.all_to_all(copies, axis, split_axis=0, concat_axis=0, tiled=True)


def member(z, y, core):
    return ((z % SIDE) * SIDE + y % SIDE) * 2 + core


def spread_lines(block):
    groups = [[member(z, y, 0) for y in range(SIDE)] for z in range(SIDE)]
    groups += [[member(z, y, 1) for z in range(SIDE)] for y in range(SIDE)]
    copies = jnp.broadcast_to(block[None], (SIDE,) + block.shape)
    return lax.all_to_all(
        copies, PLANE, split_axis=0, concat_axis=0, axis_index_groups=groups, tiled=True
    )


def across(array, step):
    pairs = []
    for z in range(SIDE):
        for y in range(SIDE):
            pairs.append((member(z, y, 0), member(z + step, y, 0)))
            pairs.append((member(z, y, 1), member(z, y + step, 1)))
    return lax.ppermute(array, PLANE, pairs)


def ring_step(blocks):
    return across(blocks[0], -1), across(blocks[1], 1)


HERE = pl.BlockSpec(memory_space=pltpu.VMEM)
SCALAR = pl.BlockSpec(memory_space=pltpu.SMEM)
PARAMS = pltpu.CompilerParams(vmem_limit_bytes=VMEM_BYTES)


def turn(load, out, width):
    half = LANES // 2
    rows = out.shape[0]
    lower = lax.broadcasted_iota(jnp.int32, (rows, LANES), 1) < half
    for p in range(0, SIDE, 2):
        for q in range(0, SIDE, 2):
            left = load((p * SIDE + q) * half)
            right = load(((p + 1) * SIDE + q) * half)
            first = jnp.where(lower, left, pltpu.roll(right, half, 1))
            second = jnp.where(lower, pltpu.roll(left, half, 1), right)
            for offset, value in ((0, first), (1, second)):
                at = ((q + offset) * SIDE + p) * half
                out[:, at : at + LANES] = value.astype(out.dtype)


def keep(load, out, width):
    for at in range(0, width, LANES):
        out[:, at : at + LANES] = load(at).astype(out.dtype)


def turn_kernel(turned, rows, out):
    width = SIDE * SIDE * LANES // 2

    def load(at):
        return rows[:, at : at + LANES].astype(jnp.float32)

    @pl.when(turned[0] == 1)
    def _():
        turn(load, out, width)

    @pl.when(turned[0] == 0)
    def _():
        keep(load, out, width)

    out[:, width:] = rows[:, width:]


def turn_rows(rows, turned):
    return pl.pallas_call(
        turn_kernel,
        out_shape=jax.ShapeDtypeStruct(rows.shape, rows.dtype),
        in_specs=[SCALAR, HERE],
        out_specs=HERE,
        compiler_params=PARAMS,
        name="turn_rows",
    )(turned, rows)


def add_products(ring_at, near, far, total, blocks, steps, projection, first):
    half = near.shape[0]
    span = SIDE * ROWS
    for index, (block, step) in enumerate(zip(blocks, steps)):
        place = lax.rem(ring_at[0] + step, SIDE) * span
        chunk = pl.ds(pl.multiple_of(place, span), span)
        for part, rows in enumerate((near, far)):
            here = slice(part * half, (part + 1) * half)
            term = jnp.dot(
                rows[:, chunk], block[:, :projection], preferred_element_type=jnp.float32
            )
            if first and index == 0:
                total[here, :] = term
            else:
                total[here, :] += term


def collect(blocks, out_rows, projection):
    start = 0
    for block in blocks:
        out_rows[start : start + block.shape[0], :] = block[:, projection:]
        start += block.shape[0]


def project_kernel(steps, ring_at, near, far, *rest):
    blocks, total, out_rows = rest[: len(steps)], rest[-2], rest[-1]
    projection = total.shape[1]
    first = len(rest) == len(steps) + 2
    collect(blocks, out_rows, projection)
    if not first:
        total[...] = rest[-3][...]
    add_products(ring_at, near, far, total, blocks, steps, projection, first)


def project(ring_at, near, far, blocks, steps, projection, so_far=None):
    rows, depth = 2 * near.shape[0], sum(block.shape[0] for block in blocks)
    columns = blocks[0].shape[1]
    operands = (ring_at, near, far, *blocks) + (() if so_far is None else (so_far,))
    return pl.pallas_call(
        functools.partial(project_kernel, steps),
        out_shape=[
            jax.ShapeDtypeStruct((rows, projection), jnp.float32),
            jax.ShapeDtypeStruct((depth, columns - projection), jnp.bfloat16),
        ],
        in_specs=[SCALAR] + [HERE] * (len(operands) - 1),
        out_specs=[HERE, HERE],
        compiler_params=PARAMS,
        cost_estimate=pl.CostEstimate(
            flops=2 * rows * depth * projection,
            bytes_accessed=2 * depth * (rows + columns),
            transcendentals=0,
        ),
        name="project",
    )(*operands)


def attention_kernel(
    steps, ring_at, near, far, doc_column, doc_row, place_column, place_row, so_far, *rest
):
    blocks, (attended, out_rows, total, held) = rest[: len(steps)], rest[len(steps) :]
    half = near.shape[0]
    projection = held.shape[1]
    group = attended.shape[1] // HEAD_DIM
    halves = [slice(0, half), slice(half, 2 * half)]
    collect(blocks, out_rows, projection)
    total[...] = so_far[...]
    add_products(ring_at, near, far, total, blocks, steps, projection, False)
    held[...] = total[...].astype(jnp.bfloat16)
    key_at = group * HEAD_DIM
    keys = held[:, key_at : key_at + HEAD_DIM]
    values = held[:, key_at + HEAD_DIM : key_at + 2 * HEAD_DIM]
    scale = HEAD_DIM**-0.5 * math.log2(math.e)
    for here in halves:
        same = doc_column[here, :] == doc_row[...]
        allowed = same & (place_column[here, :] >= place_row[...])
        hidden = jnp.where(allowed, 0.0, -1e30)
        for head in range(group):
            lanes = slice(head * HEAD_DIM, (head + 1) * HEAD_DIM)
            scores = lax.dot_general(
                held[here, lanes], keys, (((1,), (1,)), ((), ())), preferred_element_type=jnp.float32
            )
            scores = scores * scale + hidden
            weight = jnp.exp2(scores - jnp.max(scores, axis=1, keepdims=True))
            share = 1.0 / jnp.sum(weight, axis=1, keepdims=True)
            mixed = jnp.dot(weight.astype(jnp.bfloat16), values, preferred_element_type=jnp.float32)
            attended[here, lanes] = (mixed * share).astype(jnp.bfloat16)


def attention(ring_at, near, far, docs, places, so_far, blocks, steps, head_columns):
    rows, projection = so_far.shape
    depth = sum(block.shape[0] for block in blocks)
    columns = blocks[0].shape[1]
    masks = (docs[:, None], docs[None, :], places[:, None], places[None, :])
    return pl.pallas_call(
        functools.partial(attention_kernel, steps),
        out_shape=[
            jax.ShapeDtypeStruct((rows, head_columns), jnp.bfloat16),
            jax.ShapeDtypeStruct((depth, columns - projection), jnp.bfloat16),
        ],
        in_specs=[SCALAR] + [HERE] * (7 + len(blocks)),
        out_specs=[HERE, HERE],
        scratch_shapes=[
            pltpu.VMEM((rows, projection), jnp.float32),
            pltpu.VMEM((rows, projection), jnp.bfloat16),
        ],
        compiler_params=PARAMS,
        cost_estimate=pl.CostEstimate(
            flops=2 * rows * depth * projection + 4 * rows * rows * head_columns,
            bytes_accessed=2 * depth * columns + 8 * rows * projection,
            transcendentals=rows * rows * head_columns // HEAD_DIM,
        ),
        name="attention",
    )(ring_at, near, far, *masks, so_far, *blocks)


def output_kernel(first, turned, steps, ring_at, attended, *rest):
    pieces, out, held = rest[:-2], rest[-2], rest[-1]
    rows = out.shape[0]
    span = SIDE * ROWS
    result = held if turned else out
    index = 0
    for piece in pieces:
        for start in range(0, piece.shape[0], span):
            term = lax.dot_general(
                attended[first : first + rows, :],
                piece[start : start + span, :],
                (((1,), (1,)), ((), ())),
                preferred_element_type=jnp.float32,
            )
            place = lax.rem(ring_at[0] + steps[index], SIDE) * span
            result[:, pl.ds(pl.multiple_of(place, span), span)] = term.astype(result.dtype)
            index += 1
    if turned:
        turn(lambda at: held[:, at : at + LANES], out, out.shape[1])


def output_half(first, rows, turned, ring_at, attended, pieces, steps):
    columns = sum(piece.shape[0] for piece in pieces)
    held = pltpu.VMEM((rows, columns) if turned else (8, LANES), jnp.float32)
    return pl.pallas_call(
        functools.partial(output_kernel, first, turned, steps),
        out_shape=jax.ShapeDtypeStruct((rows, columns), jnp.bfloat16),
        in_specs=[SCALAR] + [HERE] * (1 + len(pieces)),
        out_specs=HERE,
        scratch_shapes=[held],
        compiler_params=PARAMS,
        cost_estimate=pl.CostEstimate(
            flops=2 * rows * columns * attended.shape[1],
            bytes_accessed=2 * columns * (rows + attended.shape[1]),
            transcendentals=0,
        ),
        name="output_product",
    )(ring_at, attended, *pieces)


def finish_kernel(turned, parts, out):
    count = parts.shape[0]

    def load(at):
        total = parts[0, :, at : at + LANES].astype(jnp.float32)
        for part in range(1, count):
            total = total + parts[part, :, at : at + LANES].astype(jnp.float32)
        return total

    @pl.when(turned[0] == 1)
    def _():
        turn(load, out, out.shape[1])

    @pl.when(turned[0] == 0)
    def _():
        keep(load, out, out.shape[1])


def finish(parts, turned):
    return pl.pallas_call(
        finish_kernel,
        out_shape=jax.ShapeDtypeStruct(parts.shape[1:], jnp.bfloat16),
        in_specs=[SCALAR, HERE],
        out_specs=HERE,
        compiler_params=PARAMS,
        name="finish",
    )(turned, parts)


def on_device(tokens, repack_plan, document_ids, norm_gain, w_query, w_key, w_value, w_out):
    row_count, width = tokens.shape
    x_count = lax.axis_size("x")
    peer_count = SIDE * SIDE
    core_index = lax.axis_index("core").astype(jnp.int32)
    ring_at = jnp.where(core_index == 0, lax.axis_index("z"), lax.axis_index("y"))
    ring_at = ring_at.astype(jnp.int32).reshape(1)
    turned = core_index.reshape(1)
    pack_rows = row_count * x_count * 2
    projection = w_query.shape[1] + w_key.shape[1] + w_value.shape[1]
    positions = jnp.arange(row_count, dtype=jnp.int32)

    with jax.named_scope("weights_spread"):
        own_weights = jnp.concatenate([w_query, w_key, w_value, w_out.T], axis=1)
        line = spread_lines(own_weights).reshape(SIDE * row_count, -1)

    with jax.named_scope("dispatch"):
        capacity = 2
        slot_count = peer_count * capacity
        target = repack_plan // pack_rows
        landing = repack_plan % row_count
        same_pack = target[:, None] == target[None, :]
        earlier = positions[None, :] < positions[:, None]
        slot_rank = jnp.sum(jnp.where(same_pack & earlier, 1, 0), axis=1).astype(jnp.int32)
        slot_of = target * capacity + slot_rank
        selector = slot_of[None, :] == jnp.arange(slot_count, dtype=jnp.int32)[:, None]
        marks = jnp.broadcast_to((landing + 1)[:, None], (row_count, LANES)).astype(jnp.bfloat16)
        outgoing = jnp.dot(
            selector.astype(jnp.bfloat16),
            jnp.concatenate([tokens, marks], axis=1),
            preferred_element_type=jnp.float32,
        ).astype(jnp.bfloat16)
        line, outgoing = lax.optimization_barrier((line, outgoing))
        line_1 = ring_step((line, line))
        arrived = lax.all_to_all(outgoing, ("z", "y"), split_axis=0, concat_axis=0, tiled=True)
        arrived_marks = arrived[:, width].astype(jnp.int32)
        settle = arrived_marks[None, :] == positions[:, None] + 1
        owned = jnp.dot(
            settle.astype(jnp.bfloat16), arrived[:, :width], preferred_element_type=jnp.float32
        ).astype(jnp.bfloat16)
        normed_own = rms_rows(owned, norm_gain)

    with jax.named_scope("pack_rows"):
        doc_columns = jnp.broadcast_to(document_ids[:, None], (row_count, LANES))
        labelled = jnp.concatenate([normed_own, doc_columns.astype(jnp.bfloat16)], axis=1)
        labelled = turn_rows(labelled, turned)
        line_1, _ = lax.optimization_barrier((line_1, labelled))
        line_2 = ring_step(line_1)
        line_3 = ring_step(line_2)
        near = spread(labelled, "x").reshape(x_count * row_count, -1)
        near, _ = lax.optimization_barrier((near, line_2[0]))
        far = shift(turn_rows(near, jnp.ones((1,), jnp.int32)), "core", 1)
        line_4 = (across(line_3[0], -1),)
        far, _ = lax.optimization_barrier((far, line_3))
        docs = jnp.concatenate([near[:, width], far[:, width]]).astype(jnp.int32)
        even = 2 * jnp.arange(x_count, dtype=jnp.int32)
        block_of = jnp.concatenate([even + core_index, even + 1 - core_index])
        places = (block_of[:, None] * row_count + positions[None, :]).reshape(pack_rows)

    with jax.named_scope("attention"):
        early, early_steps = [line, *line_1, *line_2], (0, 1, 7, 2, 6)
        so_far, pieces = project(ring_at, near, far, early, early_steps, projection)
        so_far, pieces_3 = project(ring_at, near, far, line_3, (3, 5), projection, so_far)
        attended, pieces_4 = attention(
            ring_at, near, far, docs, places, so_far, line_4, (4,), w_query.shape[1]
        )

    with jax.named_scope("output"):
        half = x_count * row_count
        pieces = (pieces, pieces_3, pieces_4)
        steps = early_steps + (3, 5, 4)
        theirs = output_half(half, half, True, ring_at, attended, pieces, steps)
        received = shift(theirs, "core", 1)
        ours = output_half(0, half, False, ring_at, attended, pieces, steps)
        both = (ours.astype(jnp.float32) + received.astype(jnp.float32)).astype(jnp.bfloat16)
        parts = lax.all_to_all(both, "x", split_axis=0, concat_axis=0, tiled=True)
        return finish(parts.reshape(x_count, row_count, -1), turned)


def solution(mesh):
    grid = Mesh(mesh.devices.reshape(SIDE, SIDE, 4, 2), ("z", "y", "x", "core"))
    dp, tensor, rows = ("z", "y"), ("x", "core"), ("z", "y", "x", "core")
    return jax.shard_map(
        on_device,
        mesh=grid,
        in_specs=(
            P(rows, None),
            P(rows),
            P(rows),
            P(),
            P(dp, tensor),
            P(dp, tensor),
            P(dp, tensor),
            P(tensor, dp),
        ),
        out_specs=P(rows, None),
        check_vma=False,
    )
```

```python
import functools
import math

import jax
import jax.numpy as jnp
from jax import lax
from jax.experimental import pallas as pl
from jax.experimental.pallas import tpu as pltpu
from jax.sharding import Mesh, PartitionSpec as P

HEAD_DIM = 128
LANES = 128
SIDE = 8
ROWS = 64
VMEM_BYTES = 16 * 1024 * 1024
PLANE = ("z", "y", "core")


def rms_rows(states, norm_gain):
    floats = states.astype(jnp.float32)
    mean_square = jnp.mean(floats * floats, axis=-1, keepdims=True)
    return (floats * lax.rsqrt(mean_square + 1e-05) * norm_gain).astype(jnp.bfloat16)


def shift(array, axis, step):
    size = lax.axis_size(axis)
    return lax.ppermute(array, axis, [(i, (i + step) % size) for i in range(size)])


def spread(block, axis):
    size = lax.axis_size(axis)
    copies = jnp.broadcast_to(block[None], (size,) + block.shape)
    return lax.all_to_all(copies, axis, split_axis=0, concat_axis=0, tiled=True)


def member(z, y, core):
    return ((z % SIDE) * SIDE + y % SIDE) * 2 + core


def spread_lines(block):
    groups = [[member(z, y, 0) for y in range(SIDE)] for z in range(SIDE)]
    groups += [[member(z, y, 1) for z in range(SIDE)] for y in range(SIDE)]
    copies = jnp.broadcast_to(block[None], (SIDE,) + block.shape)
    return lax.all_to_all(
        copies, PLANE, split_axis=0, concat_axis=0, axis_index_groups=groups, tiled=True
    )


def across(array, step):
    pairs = []
    for z in range(SIDE):
        for y in range(SIDE):
            pairs.append((member(z, y, 0), member(z + step, y, 0)))
            pairs.append((member(z, y, 1), member(z, y + step, 1)))
    return lax.ppermute(array, PLANE, pairs)


def ring_step(blocks):
    return across(blocks[0], -1), across(blocks[1], 1)


HERE = pl.BlockSpec(memory_space=pltpu.VMEM)
SCALAR = pl.BlockSpec(memory_space=pltpu.SMEM)
PARAMS = pltpu.CompilerParams(vmem_limit_bytes=VMEM_BYTES)


def turn(load, out, width):
    half = LANES // 2
    rows = out.shape[0]
    lower = lax.broadcasted_iota(jnp.int32, (rows, LANES), 1) < half
    for p in range(0, SIDE, 2):
        for q in range(0, SIDE, 2):
            left = load((p * SIDE + q) * half)
            right = load(((p + 1) * SIDE + q) * half)
            first = jnp.where(lower, left, pltpu.roll(right, half, 1))
            second = jnp.where(lower, pltpu.roll(left, half, 1), right)
            for offset, value in ((0, first), (1, second)):
                at = ((q + offset) * SIDE + p) * half
                out[:, at : at + LANES] = value.astype(out.dtype)


def keep(load, out, width):
    for at in range(0, width, LANES):
        out[:, at : at + LANES] = load(at).astype(out.dtype)


def turn_kernel(turned, rows, out):
    width = SIDE * SIDE * LANES // 2

    def load(at):
        return rows[:, at : at + LANES].astype(jnp.float32)

    @pl.when(turned[0] == 1)
    def _():
        turn(load, out, width)

    @pl.when(turned[0] == 0)
    def _():
        keep(load, out, width)

    out[:, width:] = rows[:, width:]


def turn_rows(rows, turned):
    return pl.pallas_call(
        turn_kernel,
        out_shape=jax.ShapeDtypeStruct(rows.shape, rows.dtype),
        in_specs=[SCALAR, HERE],
        out_specs=HERE,
        compiler_params=PARAMS,
        name="turn_rows",
    )(turned, rows)


def add_products(ring_at, near, far, total, blocks, steps, projection, first):
    half = near.shape[0]
    span = SIDE * ROWS
    for index, (block, step) in enumerate(zip(blocks, steps)):
        place = lax.rem(ring_at[0] + step, SIDE) * span
        chunk = pl.ds(pl.multiple_of(place, span), span)
        for part, rows in enumerate((near, far)):
            here = slice(part * half, (part + 1) * half)
            term = jnp.dot(
                rows[:, chunk], block[:, :projection], preferred_element_type=jnp.float32
            )
            if first and index == 0:
                total[here, :] = term
            else:
                total[here, :] += term


def collect(blocks, out_rows, projection):
    start = 0
    for block in blocks:
        out_rows[start : start + block.shape[0], :] = block[:, projection:]
        start += block.shape[0]


def project_kernel(steps, ring_at, near, far, *rest):
    first = len(rest) == len(steps) + 2
    blocks = rest[: len(steps)]
    if first:
        total, out_rows = rest[len(steps) :]
    else:
        so_far, total, out_rows, last_rows = rest[len(steps) :]
        total[...] = so_far[...]
        half, span = near.shape[0], SIDE * ROWS
        place = lax.rem(ring_at[0] + SIDE // 2, SIDE) * span
        chunk = pl.ds(pl.multiple_of(place, span), span)
        last_rows[:half, :] = near[:, chunk]
        last_rows[half:, :] = far[:, chunk]
    projection = total.shape[1]
    collect(blocks, out_rows, projection)
    add_products(ring_at, near, far, total, blocks, steps, projection, first)


def project(ring_at, near, far, blocks, steps, projection, so_far=None):
    rows, depth = 2 * near.shape[0], sum(block.shape[0] for block in blocks)
    columns = blocks[0].shape[1]
    operands = (ring_at, near, far, *blocks)
    results = [
        jax.ShapeDtypeStruct((rows, projection), jnp.float32),
        jax.ShapeDtypeStruct((depth, columns - projection), jnp.bfloat16),
    ]
    if so_far is not None:
        operands += (so_far,)
        results.append(jax.ShapeDtypeStruct((rows, SIDE * ROWS), jnp.bfloat16))
    return pl.pallas_call(
        functools.partial(project_kernel, steps),
        out_shape=results,
        in_specs=[SCALAR] + [HERE] * (len(operands) - 1),
        out_specs=[HERE] * len(results),
        compiler_params=PARAMS,
        cost_estimate=pl.CostEstimate(
            flops=2 * rows * depth * projection,
            bytes_accessed=2 * depth * (rows + columns),
            transcendentals=0,
        ),
        name="project",
    )(*operands)


def attention_kernel(
    rows, doc_column, doc_row, place_column, place_row, so_far, block, attended, held
):
    half = rows.shape[0] // 2
    group = attended.shape[1] // HEAD_DIM
    halves = [slice(0, half), slice(half, 2 * half)]
    for here in halves:
        term = jnp.dot(
            rows[here, :], block[...], preferred_element_type=jnp.float32
        )
        held[here, :] = (so_far[here, :] + term).astype(jnp.bfloat16)
    key_at = group * HEAD_DIM
    keys = held[:, key_at : key_at + HEAD_DIM]
    values = held[:, key_at + HEAD_DIM : key_at + 2 * HEAD_DIM]
    scale = HEAD_DIM**-0.5 * math.log2(math.e)
    for here in halves:
        same = doc_column[here, :] == doc_row[...]
        allowed = same & (place_column[here, :] >= place_row[...])
        hidden = jnp.where(allowed, 0.0, -1e30)
        for head in range(group):
            lanes = slice(head * HEAD_DIM, (head + 1) * HEAD_DIM)
            scores = lax.dot_general(
                held[here, lanes], keys, (((1,), (1,)), ((), ())), preferred_element_type=jnp.float32
            )
            scores = scores * scale + hidden
            weight = jnp.exp2(scores - jnp.max(scores, axis=1, keepdims=True))
            share = 1.0 / jnp.sum(weight, axis=1, keepdims=True)
            mixed = jnp.dot(weight.astype(jnp.bfloat16), values, preferred_element_type=jnp.float32)
            attended[here, lanes] = (mixed * share).astype(jnp.bfloat16)


def attention(last_rows, docs, places, so_far, block, head_columns):
    rows, projection = so_far.shape
    depth = block.shape[0]
    masks = (docs[:, None], docs[None, :], places[:, None], places[None, :])
    return pl.pallas_call(
        attention_kernel,
        out_shape=jax.ShapeDtypeStruct((rows, head_columns), jnp.bfloat16),
        in_specs=[HERE] * 7,
        out_specs=HERE,
        scratch_shapes=[pltpu.VMEM((rows, projection), jnp.bfloat16)],
        compiler_params=PARAMS,
        cost_estimate=pl.CostEstimate(
            flops=2 * rows * depth * projection + 4 * rows * rows * head_columns,
            bytes_accessed=2 * depth * projection + 8 * rows * projection,
            transcendentals=rows * rows * head_columns // HEAD_DIM,
        ),
        name="attention",
    )(last_rows, *masks, so_far, block)


def output_kernel(first, turned, steps, ring_at, attended, *rest):
    pieces, out, held = rest[:-2], rest[-2], rest[-1]
    rows = out.shape[0]
    span = SIDE * ROWS
    result = held if turned else out
    index = 0
    for piece in pieces:
        for start in range(0, piece.shape[0], span):
            term = lax.dot_general(
                attended[first : first + rows, :],
                piece[start : start + span, :],
                (((1,), (1,)), ((), ())),
                preferred_element_type=jnp.float32,
            )
            place = lax.rem(ring_at[0] + steps[index], SIDE) * span
            result[:, pl.ds(pl.multiple_of(place, span), span)] = term.astype(result.dtype)
            index += 1
    if turned:
        turn(lambda at: held[:, at : at + LANES], out, out.shape[1])


def output_half(first, rows, turned, ring_at, attended, pieces, steps):
    columns = sum(piece.shape[0] for piece in pieces)
    held = pltpu.VMEM((rows, columns) if turned else (8, LANES), jnp.float32)
    return pl.pallas_call(
        functools.partial(output_kernel, first, turned, steps),
        out_shape=jax.ShapeDtypeStruct((rows, columns), jnp.bfloat16),
        in_specs=[SCALAR] + [HERE] * (1 + len(pieces)),
        out_specs=HERE,
        scratch_shapes=[held],
        compiler_params=PARAMS,
        cost_estimate=pl.CostEstimate(
            flops=2 * rows * columns * attended.shape[1],
            bytes_accessed=2 * columns * (rows + attended.shape[1]),
            transcendentals=0,
        ),
        name="output_product",
    )(ring_at, attended, *pieces)


def finish_kernel(turned, parts, out):
    count = parts.shape[0]

    def load(at):
        total = parts[0, :, at : at + LANES].astype(jnp.float32)
        for part in range(1, count):
            total = total + parts[part, :, at : at + LANES].astype(jnp.float32)
        return total

    @pl.when(turned[0] == 1)
    def _():
        turn(load, out, out.shape[1])

    @pl.when(turned[0] == 0)
    def _():
        keep(load, out, out.shape[1])


def finish(parts, turned):
    return pl.pallas_call(
        finish_kernel,
        out_shape=jax.ShapeDtypeStruct(parts.shape[1:], jnp.bfloat16),
        in_specs=[SCALAR, HERE],
        out_specs=HERE,
        compiler_params=PARAMS,
        name="finish",
    )(turned, parts)


def on_device(tokens, repack_plan, document_ids, norm_gain, w_query, w_key, w_value, w_out):
    row_count, width = tokens.shape
    x_count = lax.axis_size("x")
    peer_count = SIDE * SIDE
    core_index = lax.axis_index("core").astype(jnp.int32)
    ring_at = jnp.where(core_index == 0, lax.axis_index("z"), lax.axis_index("y"))
    ring_at = ring_at.astype(jnp.int32).reshape(1)
    turned = core_index.reshape(1)
    pack_rows = row_count * x_count * 2
    projection = w_query.shape[1] + w_key.shape[1] + w_value.shape[1]
    positions = jnp.arange(row_count, dtype=jnp.int32)

    with jax.named_scope("weights_spread"):
        own_weights = jnp.concatenate([w_query, w_key, w_value, w_out.T], axis=1)
        line = spread_lines(own_weights).reshape(SIDE * row_count, -1)

    with jax.named_scope("dispatch"):
        capacity = 2
        slot_count = peer_count * capacity
        target = repack_plan // pack_rows
        landing = repack_plan % row_count
        same_pack = target[:, None] == target[None, :]
        earlier = positions[None, :] < positions[:, None]
        slot_rank = jnp.sum(jnp.where(same_pack & earlier, 1, 0), axis=1).astype(jnp.int32)
        slot_of = target * capacity + slot_rank
        selector = slot_of[None, :] == jnp.arange(slot_count, dtype=jnp.int32)[:, None]
        marks = jnp.broadcast_to((landing + 1)[:, None], (row_count, LANES)).astype(jnp.bfloat16)
        outgoing = jnp.dot(
            selector.astype(jnp.bfloat16),
            jnp.concatenate([tokens, marks], axis=1),
            preferred_element_type=jnp.float32,
        ).astype(jnp.bfloat16)
        line, outgoing = lax.optimization_barrier((line, outgoing))
        line_1 = ring_step((line, line))
        arrived = lax.all_to_all(outgoing, ("z", "y"), split_axis=0, concat_axis=0, tiled=True)
        arrived_marks = arrived[:, width].astype(jnp.int32)
        settle = arrived_marks[None, :] == positions[:, None] + 1
        owned = jnp.dot(
            settle.astype(jnp.bfloat16), arrived[:, :width], preferred_element_type=jnp.float32
        ).astype(jnp.bfloat16)
        normed_own = rms_rows(owned, norm_gain)

    with jax.named_scope("pack_rows"):
        doc_columns = jnp.broadcast_to(document_ids[:, None], (row_count, LANES))
        labelled = jnp.concatenate([normed_own, doc_columns.astype(jnp.bfloat16)], axis=1)
        labelled = turn_rows(labelled, turned)
        line_1, _ = lax.optimization_barrier((line_1, labelled))
        line_2 = ring_step(line_1)
        line_3 = ring_step(line_2)
        near = spread(labelled, "x").reshape(x_count * row_count, -1)
        near, _ = lax.optimization_barrier((near, line_2[0]))
        far = turn_rows(shift(near, "core", 1), jnp.ones((1,), jnp.int32))
        docs = jnp.concatenate([near[:, width], far[:, width]]).astype(jnp.int32)
        even = 2 * jnp.arange(x_count, dtype=jnp.int32)
        block_of = jnp.concatenate([even + core_index, even + 1 - core_index])
        places = (block_of[:, None] * row_count + positions[None, :]).reshape(pack_rows)

    with jax.named_scope("attention"):
        early, early_steps = [line, *line_1, *line_2], (0, 1, 7, 2, 6)
        so_far, pieces = project(ring_at, near, far, early, early_steps, projection)
        line_3, _ = lax.optimization_barrier((line_3, so_far))
        block_4 = across(line_3[0][:, :projection], -1)
        pieces_4 = across(line_3[1][:, projection:], 1)
        so_far, pieces_3, last_rows = project(
            ring_at, near, far, line_3, (3, 5), projection, so_far
        )
        attended = attention(last_rows, docs, places, so_far, block_4, w_query.shape[1])

    with jax.named_scope("output"):
        half = x_count * row_count
        pieces = (pieces, pieces_3, pieces_4)
        steps = early_steps + (3, 5, 4)
        theirs = output_half(half, half, True, ring_at, attended, pieces, steps)
        received = shift(theirs, "core", 1)
        ours = output_half(0, half, False, ring_at, attended, pieces, steps)
        both = (ours.astype(jnp.float32) + received.astype(jnp.float32)).astype(jnp.bfloat16)
        parts = lax.all_to_all(both, "x", split_axis=0, concat_axis=0, tiled=True)
        return finish(parts.reshape(x_count, row_count, -1), turned)


def solution(mesh):
    grid = Mesh(mesh.devices.reshape(SIDE, SIDE, 4, 2), ("z", "y", "x", "core"))
    dp, tensor, rows = ("z", "y"), ("x", "core"), ("z", "y", "x", "core")
    return jax.shard_map(
        on_device,
        mesh=grid,
        in_specs=(
            P(rows, None),
            P(rows),
            P(rows),
            P(),
            P(dp, tensor),
            P(dp, tensor),
            P(dp, tensor),
            P(tensor, dp),
        ),
        out_specs=P(rows, None),
        check_vma=False,
    )
```

```python
import functools
import math

import jax
import jax.numpy as jnp
from jax import lax
from jax.experimental import pallas as pl
from jax.experimental.pallas import tpu as pltpu
from jax.sharding import Mesh, PartitionSpec as P

HEAD_DIM = 128
LANES = 128
SIDE = 8
ROWS = 64
VMEM_BYTES = 16 * 1024 * 1024
PLANE = ("z", "y", "core")


def rms_rows(states, norm_gain):
    floats = states.astype(jnp.float32)
    mean_square = jnp.mean(floats * floats, axis=-1, keepdims=True)
    return (floats * lax.rsqrt(mean_square + 1e-05) * norm_gain).astype(jnp.bfloat16)


def shift(array, axis, step):
    size = lax.axis_size(axis)
    return lax.ppermute(array, axis, [(i, (i + step) % size) for i in range(size)])


def spread(block, axis):
    size = lax.axis_size(axis)
    copies = jnp.broadcast_to(block[None], (size,) + block.shape)
    return lax.all_to_all(copies, axis, split_axis=0, concat_axis=0, tiled=True)


def member(z, y, core):
    return ((z % SIDE) * SIDE + y % SIDE) * 2 + core


def spread_lines(block):
    groups = [[member(z, y, 0) for y in range(SIDE)] for z in range(SIDE)]
    groups += [[member(z, y, 1) for z in range(SIDE)] for y in range(SIDE)]
    copies = jnp.broadcast_to(block[None], (SIDE,) + block.shape)
    return lax.all_to_all(
        copies, PLANE, split_axis=0, concat_axis=0, axis_index_groups=groups, tiled=True
    )


def across(array, step):
    pairs = []
    for z in range(SIDE):
        for y in range(SIDE):
            pairs.append((member(z, y, 0), member(z + step, y, 0)))
            pairs.append((member(z, y, 1), member(z, y + step, 1)))
    return lax.ppermute(array, PLANE, pairs)


def ring_step(blocks):
    return across(blocks[0], -1), across(blocks[1], 1)


HERE = pl.BlockSpec(memory_space=pltpu.VMEM)
SCALAR = pl.BlockSpec(memory_space=pltpu.SMEM)
PARAMS = pltpu.CompilerParams(vmem_limit_bytes=VMEM_BYTES)


def turn(load, out, width):
    half = LANES // 2
    rows = out.shape[0]
    lower = lax.broadcasted_iota(jnp.int32, (rows, LANES), 1) < half
    for p in range(0, SIDE, 2):
        for q in range(0, SIDE, 2):
            left = load((p * SIDE + q) * half)
            right = load(((p + 1) * SIDE + q) * half)
            first = jnp.where(lower, left, pltpu.roll(right, half, 1))
            second = jnp.where(lower, pltpu.roll(left, half, 1), right)
            for offset, value in ((0, first), (1, second)):
                at = ((q + offset) * SIDE + p) * half
                out[:, at : at + LANES] = value.astype(out.dtype)


def keep(load, out, width):
    for at in range(0, width, LANES):
        out[:, at : at + LANES] = load(at).astype(out.dtype)


def turn_kernel(turned, rows, out):
    width = SIDE * SIDE * LANES // 2

    def load(at):
        return rows[:, at : at + LANES].astype(jnp.float32)

    @pl.when(turned[0] == 1)
    def _():
        turn(load, out, width)

    @pl.when(turned[0] == 0)
    def _():
        keep(load, out, width)

    out[:, width:] = rows[:, width:]


def turn_rows(rows, turned):
    return pl.pallas_call(
        turn_kernel,
        out_shape=jax.ShapeDtypeStruct(rows.shape, rows.dtype),
        in_specs=[SCALAR, HERE],
        out_specs=HERE,
        compiler_params=PARAMS,
        name="turn_rows",
    )(turned, rows)


def add_products(ring_at, near, far, total, blocks, steps, projection, first):
    half = near.shape[0]
    span = SIDE * ROWS
    for index, (block, step) in enumerate(zip(blocks, steps)):
        place = lax.rem(ring_at[0] + step, SIDE) * span
        chunk = pl.ds(pl.multiple_of(place, span), span)
        for part, rows in enumerate((near, far)):
            here = slice(part * half, (part + 1) * half)
            term = jnp.dot(
                rows[:, chunk], block[:, :projection], preferred_element_type=jnp.float32
            )
            if first and index == 0:
                total[here, :] = term
            else:
                total[here, :] += term


def collect(blocks, out_rows, projection):
    start = 0
    for block in blocks:
        out_rows[start : start + block.shape[0], :] = block[:, projection:]
        start += block.shape[0]


def project_kernel(steps, ring_at, near, far, *rest):
    first = len(rest) == len(steps) + 2
    blocks = rest[: len(steps)]
    if first:
        total, out_rows = rest[len(steps) :]
    else:
        so_far, total, out_rows, last_rows = rest[len(steps) :]
        total[...] = so_far[...]
        half, span = near.shape[0], SIDE * ROWS
        place = lax.rem(ring_at[0] + SIDE // 2, SIDE) * span
        chunk = pl.ds(pl.multiple_of(place, span), span)
        last_rows[:half, :] = near[:, chunk]
        last_rows[half:, :] = far[:, chunk]
    projection = total.shape[1]
    collect(blocks, out_rows, projection)
    add_products(ring_at, near, far, total, blocks, steps, projection, first)


def project(ring_at, near, far, blocks, steps, projection, so_far=None):
    rows, depth = 2 * near.shape[0], sum(block.shape[0] for block in blocks)
    columns = blocks[0].shape[1]
    operands = (ring_at, near, far, *blocks)
    results = [
        jax.ShapeDtypeStruct((rows, projection), jnp.float32),
        jax.ShapeDtypeStruct((depth, columns - projection), jnp.bfloat16),
    ]
    if so_far is not None:
        operands += (so_far,)
        results.append(jax.ShapeDtypeStruct((rows, SIDE * ROWS), jnp.bfloat16))
    return pl.pallas_call(
        functools.partial(project_kernel, steps),
        out_shape=results,
        in_specs=[SCALAR] + [HERE] * (len(operands) - 1),
        out_specs=[HERE] * len(results),
        compiler_params=PARAMS,
        cost_estimate=pl.CostEstimate(
            flops=2 * rows * depth * projection,
            bytes_accessed=2 * depth * (rows + columns),
            transcendentals=0,
        ),
        name="project",
    )(*operands)


def attend(held, first, doc_column, doc_row, place_column, place_row, attended):
    rows = attended.shape[0]
    here = slice(first, first + rows)
    group = attended.shape[1] // HEAD_DIM
    key_at = group * HEAD_DIM
    keys = held[:, key_at : key_at + HEAD_DIM]
    values = held[:, key_at + HEAD_DIM : key_at + 2 * HEAD_DIM]
    scale = HEAD_DIM**-0.5 * math.log2(math.e)
    same = doc_column[here, :] == doc_row[...]
    allowed = same & (place_column[here, :] >= place_row[...])
    hidden = jnp.where(allowed, 0.0, -1e30)
    for head in range(group):
        lanes = slice(head * HEAD_DIM, (head + 1) * HEAD_DIM)
        scores = lax.dot_general(
            held[here, lanes], keys, (((1,), (1,)), ((), ())), preferred_element_type=jnp.float32
        )
        scores = scores * scale + hidden
        weight = jnp.exp2(scores - jnp.max(scores, axis=1, keepdims=True))
        share = 1.0 / jnp.sum(weight, axis=1, keepdims=True)
        mixed = jnp.dot(weight.astype(jnp.bfloat16), values, preferred_element_type=jnp.float32)
        attended[:, lanes] = (mixed * share).astype(jnp.bfloat16)


def far_attention_kernel(rows, so_far, block, *rest):
    masks, attended, held = rest[:4], rest[4], rest[5]
    half = rows.shape[0] // 2
    for here in (slice(0, half), slice(half, 2 * half)):
        term = jnp.dot(rows[here, :], block[...], preferred_element_type=jnp.float32)
        held[here, :] = (so_far[here, :] + term).astype(jnp.bfloat16)
    attend(held, half, *masks, attended)


def near_attention_kernel(held, *rest):
    attend(held, 0, *rest)


def far_attention(last_rows, so_far, block, masks, head_columns):
    rows, projection = so_far.shape
    depth = block.shape[0]
    return pl.pallas_call(
        far_attention_kernel,
        out_shape=[
            jax.ShapeDtypeStruct((rows // 2, head_columns), jnp.bfloat16),
            jax.ShapeDtypeStruct((rows, projection), jnp.bfloat16),
        ],
        in_specs=[HERE] * 7,
        out_specs=[HERE, HERE],
        compiler_params=PARAMS,
        cost_estimate=pl.CostEstimate(
            flops=2 * rows * depth * projection + 2 * rows * rows * head_columns,
            bytes_accessed=2 * depth * projection + 8 * rows * projection,
            transcendentals=rows * rows * head_columns // HEAD_DIM // 2,
        ),
        name="far_attention",
    )(last_rows, so_far, block, *masks)


def near_attention(held, masks, head_columns):
    rows = held.shape[0]
    return pl.pallas_call(
        near_attention_kernel,
        out_shape=jax.ShapeDtypeStruct((rows // 2, head_columns), jnp.bfloat16),
        in_specs=[HERE] * 5,
        out_specs=HERE,
        compiler_params=PARAMS,
        cost_estimate=pl.CostEstimate(
            flops=2 * rows * rows * head_columns,
            bytes_accessed=2 * held.size,
            transcendentals=rows * rows * head_columns // HEAD_DIM // 2,
        ),
        name="near_attention",
    )(held, *masks)


def output_kernel(turned, steps, ring_at, attended, *rest):
    pieces, out, held = rest[:-2], rest[-2], rest[-1]
    rows = out.shape[0]
    span = SIDE * ROWS
    result = held if turned else out
    index = 0
    for piece in pieces:
        for start in range(0, piece.shape[0], span):
            term = lax.dot_general(
                attended[...],
                piece[start : start + span, :],
                (((1,), (1,)), ((), ())),
                preferred_element_type=jnp.float32,
            )
            place = lax.rem(ring_at[0] + steps[index], SIDE) * span
            result[:, pl.ds(pl.multiple_of(place, span), span)] = term.astype(result.dtype)
            index += 1
    if turned:
        turn(lambda at: held[:, at : at + LANES], out, out.shape[1])


def output_half(rows, turned, ring_at, attended, pieces, steps):
    columns = sum(piece.shape[0] for piece in pieces)
    held = pltpu.VMEM((rows, columns) if turned else (8, LANES), jnp.float32)
    return pl.pallas_call(
        functools.partial(output_kernel, turned, steps),
        out_shape=jax.ShapeDtypeStruct((rows, columns), jnp.bfloat16),
        in_specs=[SCALAR] + [HERE] * (1 + len(pieces)),
        out_specs=HERE,
        scratch_shapes=[held],
        compiler_params=PARAMS,
        cost_estimate=pl.CostEstimate(
            flops=2 * rows * columns * attended.shape[1],
            bytes_accessed=2 * columns * (rows + attended.shape[1]),
            transcendentals=0,
        ),
        name="output_product",
    )(ring_at, attended, *pieces)


def finish_kernel(turned, parts, out):
    count = parts.shape[0]

    def load(at):
        total = parts[0, :, at : at + LANES].astype(jnp.float32)
        for part in range(1, count):
            total = total + parts[part, :, at : at + LANES].astype(jnp.float32)
        return total

    @pl.when(turned[0] == 1)
    def _():
        turn(load, out, out.shape[1])

    @pl.when(turned[0] == 0)
    def _():
        keep(load, out, out.shape[1])


def finish(parts, turned):
    return pl.pallas_call(
        finish_kernel,
        out_shape=jax.ShapeDtypeStruct(parts.shape[1:], jnp.bfloat16),
        in_specs=[SCALAR, HERE],
        out_specs=HERE,
        compiler_params=PARAMS,
        name="finish",
    )(turned, parts)


def on_device(tokens, repack_plan, document_ids, norm_gain, w_query, w_key, w_value, w_out):
    row_count, width = tokens.shape
    x_count = lax.axis_size("x")
    peer_count = SIDE * SIDE
    core_index = lax.axis_index("core").astype(jnp.int32)
    ring_at = jnp.where(core_index == 0, lax.axis_index("z"), lax.axis_index("y"))
    ring_at = ring_at.astype(jnp.int32).reshape(1)
    turned = core_index.reshape(1)
    pack_rows = row_count * x_count * 2
    projection = w_query.shape[1] + w_key.shape[1] + w_value.shape[1]
    positions = jnp.arange(row_count, dtype=jnp.int32)

    with jax.named_scope("weights_spread"):
        own_weights = jnp.concatenate([w_query, w_key, w_value, w_out.T], axis=1)
        line = spread_lines(own_weights).reshape(SIDE * row_count, -1)

    with jax.named_scope("dispatch"):
        capacity = 2
        slot_count = peer_count * capacity
        target = repack_plan // pack_rows
        landing = repack_plan % row_count
        same_pack = target[:, None] == target[None, :]
        earlier = positions[None, :] < positions[:, None]
        slot_rank = jnp.sum(jnp.where(same_pack & earlier, 1, 0), axis=1).astype(jnp.int32)
        slot_of = target * capacity + slot_rank
        selector = slot_of[None, :] == jnp.arange(slot_count, dtype=jnp.int32)[:, None]
        marks = jnp.broadcast_to((landing + 1)[:, None], (row_count, LANES)).astype(jnp.bfloat16)
        outgoing = jnp.dot(
            selector.astype(jnp.bfloat16),
            jnp.concatenate([tokens, marks], axis=1),
            preferred_element_type=jnp.float32,
        ).astype(jnp.bfloat16)
        line, outgoing = lax.optimization_barrier((line, outgoing))
        line_1 = ring_step((line, line))
        arrived = lax.all_to_all(outgoing, ("z", "y"), split_axis=0, concat_axis=0, tiled=True)
        arrived_marks = arrived[:, width].astype(jnp.int32)
        settle = arrived_marks[None, :] == positions[:, None] + 1
        owned = jnp.dot(
            settle.astype(jnp.bfloat16), arrived[:, :width], preferred_element_type=jnp.float32
        ).astype(jnp.bfloat16)
        normed_own = rms_rows(owned, norm_gain)

    with jax.named_scope("pack_rows"):
        doc_columns = jnp.broadcast_to(document_ids[:, None], (row_count, LANES))
        labelled = jnp.concatenate([normed_own, doc_columns.astype(jnp.bfloat16)], axis=1)
        labelled = turn_rows(labelled, turned)
        line_1, _ = lax.optimization_barrier((line_1, labelled))
        line_2 = ring_step(line_1)
        line_3 = ring_step(line_2)
        near = spread(labelled, "x").reshape(x_count * row_count, -1)
        near, _ = lax.optimization_barrier((near, line_2[0]))
        far = turn_rows(shift(near, "core", 1), jnp.ones((1,), jnp.int32))
        docs = jnp.concatenate([near[:, width], far[:, width]]).astype(jnp.int32)
        even = 2 * jnp.arange(x_count, dtype=jnp.int32)
        block_of = jnp.concatenate([even + core_index, even + 1 - core_index])
        places = (block_of[:, None] * row_count + positions[None, :]).reshape(pack_rows)

    with jax.named_scope("attention"):
        early, early_steps = [line, *line_1, *line_2], (0, 1, 7, 2, 6)
        so_far, pieces = project(ring_at, near, far, early, early_steps, projection)
        line_3, _ = lax.optimization_barrier((line_3, so_far))
        block_4 = across(line_3[0][:, :projection], -1)
        pieces_4 = across(line_3[1][:, projection:], 1)
        so_far, pieces_3, last_rows = project(
            ring_at, near, far, line_3, (3, 5), projection, so_far
        )
        masks = (docs[:, None], docs[None, :], places[:, None], places[None, :])
        attended_far, held = far_attention(
            last_rows, so_far, block_4, masks, w_query.shape[1]
        )

    with jax.named_scope("output"):
        half = x_count * row_count
        pieces = (pieces, pieces_3, pieces_4)
        steps = early_steps + (3, 5, 4)
        theirs = output_half(half, True, ring_at, attended_far, pieces, steps)
        theirs, held = lax.optimization_barrier((theirs, held))
        received = shift(theirs, "core", 1)
        attended_near = near_attention(held, masks, w_query.shape[1])
        ours = output_half(half, False, ring_at, attended_near, pieces, steps)
        both = (ours.astype(jnp.float32) + received.astype(jnp.float32)).astype(jnp.bfloat16)
        parts = lax.all_to_all(both, "x", split_axis=0, concat_axis=0, tiled=True)
        return finish(parts.reshape(x_count, row_count, -1), turned)


def solution(mesh):
    grid = Mesh(mesh.devices.reshape(SIDE, SIDE, 4, 2), ("z", "y", "x", "core"))
    dp, tensor, rows = ("z", "y"), ("x", "core"), ("z", "y", "x", "core")
    return jax.shard_map(
        on_device,
        mesh=grid,
        in_specs=(
            P(rows, None),
            P(rows),
            P(rows),
            P(),
            P(dp, tensor),
            P(dp, tensor),
            P(dp, tensor),
            P(tensor, dp),
        ),
        out_specs=P(rows, None),
        check_vma=False,
    )
```

```python
import functools
import math

import jax
import jax.numpy as jnp
from jax import lax
from jax.experimental import pallas as pl
from jax.experimental.pallas import tpu as pltpu
from jax.sharding import Mesh, PartitionSpec as P

HEAD_DIM = 128
LANES = 128
SIDE = 8
ROWS = 64
VMEM_BYTES = 16 * 1024 * 1024
PLANE = ("z", "y", "core")


def rms_rows(states, norm_gain):
    floats = states.astype(jnp.float32)
    mean_square = jnp.mean(floats * floats, axis=-1, keepdims=True)
    return (floats * lax.rsqrt(mean_square + 1e-05) * norm_gain).astype(jnp.bfloat16)


def shift(array, axis, step):
    size = lax.axis_size(axis)
    return lax.ppermute(array, axis, [(i, (i + step) % size) for i in range(size)])


def spread(block, axis):
    size = lax.axis_size(axis)
    copies = jnp.broadcast_to(block[None], (size,) + block.shape)
    return lax.all_to_all(copies, axis, split_axis=0, concat_axis=0, tiled=True)


def member(z, y, core):
    return ((z % SIDE) * SIDE + y % SIDE) * 2 + core


def spread_lines(block):
    groups = [[member(z, y, 0) for y in range(SIDE)] for z in range(SIDE)]
    groups += [[member(z, y, 1) for z in range(SIDE)] for y in range(SIDE)]
    copies = jnp.broadcast_to(block[None], (SIDE,) + block.shape)
    return lax.all_to_all(
        copies, PLANE, split_axis=0, concat_axis=0, axis_index_groups=groups, tiled=True
    )


def across(array, step):
    pairs = []
    for z in range(SIDE):
        for y in range(SIDE):
            pairs.append((member(z, y, 0), member(z + step, y, 0)))
            pairs.append((member(z, y, 1), member(z, y + step, 1)))
    return lax.ppermute(array, PLANE, pairs)


def ring_step(blocks):
    return across(blocks[0], -1), across(blocks[1], 1)


HERE = pl.BlockSpec(memory_space=pltpu.VMEM)
SCALAR = pl.BlockSpec(memory_space=pltpu.SMEM)
PARAMS = pltpu.CompilerParams(vmem_limit_bytes=VMEM_BYTES)


def turn(load, out, width):
    half = LANES // 2
    rows = out.shape[0]
    lower = lax.broadcasted_iota(jnp.int32, (rows, LANES), 1) < half
    for p in range(0, SIDE, 2):
        for q in range(0, SIDE, 2):
            left = load((p * SIDE + q) * half)
            right = load(((p + 1) * SIDE + q) * half)
            first = jnp.where(lower, left, pltpu.roll(right, half, 1))
            second = jnp.where(lower, pltpu.roll(left, half, 1), right)
            for offset, value in ((0, first), (1, second)):
                at = ((q + offset) * SIDE + p) * half
                out[:, at : at + LANES] = value.astype(out.dtype)


def keep(load, out, width):
    for at in range(0, width, LANES):
        out[:, at : at + LANES] = load(at).astype(out.dtype)


def turn_kernel(turned, rows, out):
    width = SIDE * SIDE * LANES // 2

    def load(at):
        return rows[:, at : at + LANES].astype(jnp.float32)

    @pl.when(turned[0] == 1)
    def _():
        turn(load, out, width)

    @pl.when(turned[0] == 0)
    def _():
        keep(load, out, width)

    out[:, width:] = rows[:, width:]


def turn_rows(rows, turned):
    return pl.pallas_call(
        turn_kernel,
        out_shape=jax.ShapeDtypeStruct(rows.shape, rows.dtype),
        in_specs=[SCALAR, HERE],
        out_specs=HERE,
        compiler_params=PARAMS,
        name="turn_rows",
    )(turned, rows)


def add_products(ring_at, near, far, total, blocks, steps, projection, first):
    half = near.shape[0]
    span = SIDE * ROWS
    for index, (block, step) in enumerate(zip(blocks, steps)):
        place = lax.rem(ring_at[0] + step, SIDE) * span
        chunk = pl.ds(pl.multiple_of(place, span), span)
        for part, rows in enumerate((near, far)):
            here = slice(part * half, (part + 1) * half)
            term = jnp.dot(
                rows[:, chunk], block[:, :projection], preferred_element_type=jnp.float32
            )
            if first and index == 0:
                total[here, :] = term
            else:
                total[here, :] += term


def collect(blocks, out_rows, projection):
    start = 0
    for block in blocks:
        out_rows[start : start + block.shape[0], :] = block[:, projection:]
        start += block.shape[0]


def project_kernel(steps, ring_at, near, far, *rest):
    first = len(rest) == len(steps) + 2
    blocks = rest[: len(steps)]
    if first:
        total, out_rows = rest[len(steps) :]
    else:
        so_far, total, out_rows, last_rows = rest[len(steps) :]
        total[...] = so_far[...]
        half, span = near.shape[0], SIDE * ROWS
        place = lax.rem(ring_at[0] + SIDE // 2, SIDE) * span
        chunk = pl.ds(pl.multiple_of(place, span), span)
        last_rows[:half, :] = near[:, chunk]
        last_rows[half:, :] = far[:, chunk]
    projection = total.shape[1]
    collect(blocks, out_rows, projection)
    add_products(ring_at, near, far, total, blocks, steps, projection, first)


def project(ring_at, near, far, blocks, steps, projection, so_far=None):
    rows, depth = 2 * near.shape[0], sum(block.shape[0] for block in blocks)
    columns = blocks[0].shape[1]
    operands = (ring_at, near, far, *blocks)
    results = [
        jax.ShapeDtypeStruct((rows, projection), jnp.float32),
        jax.ShapeDtypeStruct((depth, columns - projection), jnp.bfloat16),
    ]
    if so_far is not None:
        operands += (so_far,)
        results.append(jax.ShapeDtypeStruct((rows, SIDE * ROWS), jnp.bfloat16))
    return pl.pallas_call(
        functools.partial(project_kernel, steps),
        out_shape=results,
        in_specs=[SCALAR] + [HERE] * (len(operands) - 1),
        out_specs=[HERE] * len(results),
        compiler_params=PARAMS,
        cost_estimate=pl.CostEstimate(
            flops=2 * rows * depth * projection,
            bytes_accessed=2 * depth * (rows + columns),
            transcendentals=0,
        ),
        name="project",
    )(*operands)


def attend(held, first, doc_column, doc_row, place_column, place_row, attended):
    rows = attended.shape[0]
    here = slice(first, first + rows)
    group = attended.shape[1] // HEAD_DIM
    key_at = group * HEAD_DIM
    keys = held[:, key_at : key_at + HEAD_DIM]
    values = held[:, key_at + HEAD_DIM : key_at + 2 * HEAD_DIM]
    scale = HEAD_DIM**-0.5 * math.log2(math.e)
    same = doc_column[here, :] == doc_row[...]
    allowed = same & (place_column[here, :] >= place_row[...])
    hidden = jnp.where(allowed, 0.0, -1e30)
    for head in range(group):
        lanes = slice(head * HEAD_DIM, (head + 1) * HEAD_DIM)
        scores = lax.dot_general(
            held[here, lanes], keys, (((1,), (1,)), ((), ())), preferred_element_type=jnp.float32
        )
        scores = scores * scale + hidden
        weight = jnp.exp2(scores - jnp.max(scores, axis=1, keepdims=True))
        share = 1.0 / jnp.sum(weight, axis=1, keepdims=True)
        mixed = jnp.dot(weight.astype(jnp.bfloat16), values, preferred_element_type=jnp.float32)
        attended[:, lanes] = (mixed * share).astype(jnp.bfloat16)


def far_attention_kernel(rows, so_far, block, *rest):
    masks, attended, held = rest[:4], rest[4], rest[5]
    half = rows.shape[0] // 2
    for here in (slice(0, half), slice(half, 2 * half)):
        term = jnp.dot(rows[here, :], block[...], preferred_element_type=jnp.float32)
        held[here, :] = (so_far[here, :] + term).astype(jnp.bfloat16)
    attend(held, half, *masks, attended)


def near_attention_kernel(held, *rest):
    attend(held, 0, *rest)


def far_attention(last_rows, so_far, block, masks, head_columns):
    rows, projection = so_far.shape
    depth = block.shape[0]
    return pl.pallas_call(
        far_attention_kernel,
        out_shape=[
            jax.ShapeDtypeStruct((rows // 2, head_columns), jnp.bfloat16),
            jax.ShapeDtypeStruct((rows, projection), jnp.bfloat16),
        ],
        in_specs=[HERE] * 7,
        out_specs=[HERE, HERE],
        compiler_params=PARAMS,
        cost_estimate=pl.CostEstimate(
            flops=2 * rows * depth * projection + 2 * rows * rows * head_columns,
            bytes_accessed=2 * depth * projection + 8 * rows * projection,
            transcendentals=rows * rows * head_columns // HEAD_DIM // 2,
        ),
        name="far_attention",
    )(last_rows, so_far, block, *masks)


def near_attention(held, masks, head_columns):
    rows = held.shape[0]
    return pl.pallas_call(
        near_attention_kernel,
        out_shape=jax.ShapeDtypeStruct((rows // 2, head_columns), jnp.bfloat16),
        in_specs=[HERE] * 5,
        out_specs=HERE,
        compiler_params=PARAMS,
        cost_estimate=pl.CostEstimate(
            flops=2 * rows * rows * head_columns,
            bytes_accessed=2 * held.size,
            transcendentals=rows * rows * head_columns // HEAD_DIM // 2,
        ),
        name="near_attention",
    )(held, *masks)


def output_kernel(turned, steps, ring_at, attended, *rest):
    pieces, out, held = rest[:-2], rest[-2], rest[-1]
    rows = out.shape[0]
    span = SIDE * ROWS
    result = held if turned else out
    index = 0
    for piece in pieces:
        for start in range(0, piece.shape[0], span):
            term = lax.dot_general(
                attended[...],
                piece[start : start + span, :],
                (((1,), (1,)), ((), ())),
                preferred_element_type=jnp.float32,
            )
            place = lax.rem(ring_at[0] + steps[index], SIDE) * span
            result[:, pl.ds(pl.multiple_of(place, span), span)] = term.astype(result.dtype)
            index += 1
    if turned:
        turn(lambda at: held[:, at : at + LANES], out, out.shape[1])


def output_half(rows, turned, ring_at, attended, pieces, steps):
    columns = sum(piece.shape[0] for piece in pieces)
    held = pltpu.VMEM((rows, columns) if turned else (8, LANES), jnp.float32)
    return pl.pallas_call(
        functools.partial(output_kernel, turned, steps),
        out_shape=jax.ShapeDtypeStruct((rows, columns), jnp.bfloat16),
        in_specs=[SCALAR] + [HERE] * (1 + len(pieces)),
        out_specs=HERE,
        scratch_shapes=[held],
        compiler_params=PARAMS,
        cost_estimate=pl.CostEstimate(
            flops=2 * rows * columns * attended.shape[1],
            bytes_accessed=2 * columns * (rows + attended.shape[1]),
            transcendentals=0,
        ),
        name="output_product",
    )(ring_at, attended, *pieces)


def finish_kernel(turned, parts, out):
    count = parts.shape[0]

    def load(at):
        total = parts[0, :, at : at + LANES].astype(jnp.float32)
        for part in range(1, count):
            total = total + parts[part, :, at : at + LANES].astype(jnp.float32)
        return total

    @pl.when(turned[0] == 1)
    def _():
        turn(load, out, out.shape[1])

    @pl.when(turned[0] == 0)
    def _():
        keep(load, out, out.shape[1])


def finish(parts, turned):
    return pl.pallas_call(
        finish_kernel,
        out_shape=jax.ShapeDtypeStruct(parts.shape[1:], jnp.bfloat16),
        in_specs=[SCALAR, HERE],
        out_specs=HERE,
        compiler_params=PARAMS,
        name="finish",
    )(turned, parts)


def on_device(tokens, repack_plan, document_ids, norm_gain, w_query, w_key, w_value, w_out):
    row_count, width = tokens.shape
    x_count = lax.axis_size("x")
    peer_count = SIDE * SIDE
    core_index = lax.axis_index("core").astype(jnp.int32)
    ring_at = jnp.where(core_index == 0, lax.axis_index("z"), lax.axis_index("y"))
    ring_at = ring_at.astype(jnp.int32).reshape(1)
    turned = core_index.reshape(1)
    pack_rows = row_count * x_count * 2
    projection = w_query.shape[1] + w_key.shape[1] + w_value.shape[1]
    positions = jnp.arange(row_count, dtype=jnp.int32)

    with jax.named_scope("weights_spread"):
        own_weights = jnp.concatenate([w_query, w_key, w_value, w_out.T], axis=1)
        line = spread_lines(own_weights).reshape(SIDE * row_count, -1)

    with jax.named_scope("dispatch"):
        capacity = 2
        slot_count = peer_count * capacity
        target = repack_plan // pack_rows
        landing = repack_plan % row_count
        same_pack = target[:, None] == target[None, :]
        earlier = positions[None, :] < positions[:, None]
        slot_rank = jnp.sum(jnp.where(same_pack & earlier, 1, 0), axis=1).astype(jnp.int32)
        slot_of = target * capacity + slot_rank
        selector = slot_of[None, :] == jnp.arange(slot_count, dtype=jnp.int32)[:, None]
        marks = jnp.broadcast_to((landing + 1)[:, None], (row_count, LANES)).astype(jnp.bfloat16)
        outgoing = jnp.dot(
            selector.astype(jnp.bfloat16),
            jnp.concatenate([tokens, marks], axis=1),
            preferred_element_type=jnp.float32,
        ).astype(jnp.bfloat16)
        line, outgoing = lax.optimization_barrier((line, outgoing))
        line_1 = ring_step((line, line))
        arrived = lax.all_to_all(outgoing, ("z", "y"), split_axis=0, concat_axis=0, tiled=True)
        arrived_marks = arrived[:, width].astype(jnp.int32)
        settle = arrived_marks[None, :] == positions[:, None] + 1
        owned = jnp.dot(
            settle.astype(jnp.bfloat16), arrived[:, :width], preferred_element_type=jnp.float32
        ).astype(jnp.bfloat16)
        normed_own = rms_rows(owned, norm_gain)

    with jax.named_scope("pack_rows"):
        doc_columns = jnp.broadcast_to(document_ids[:, None], (row_count, LANES))
        labelled = jnp.concatenate([normed_own, doc_columns.astype(jnp.bfloat16)], axis=1)
        labelled = turn_rows(labelled, turned)
        line_1, _ = lax.optimization_barrier((line_1, labelled))
        line_2 = ring_step(line_1)
        line_3 = ring_step(line_2)
        near = spread(labelled, "x").reshape(x_count * row_count, -1)
        near, _ = lax.optimization_barrier((near, line_2[0]))
        far = turn_rows(shift(near, "core", 1), jnp.ones((1,), jnp.int32))
        docs = jnp.concatenate([near[:, width], far[:, width]]).astype(jnp.int32)
        even = 2 * jnp.arange(x_count, dtype=jnp.int32)
        block_of = jnp.concatenate([even + core_index, even + 1 - core_index])
        places = (block_of[:, None] * row_count + positions[None, :]).reshape(pack_rows)

    with jax.named_scope("attention"):
        early, early_steps = [line, *line_1, *line_2], (0, 1, 7, 2, 6)
        so_far, pieces = project(ring_at, near, far, early, early_steps, projection)
        above_3, _ = lax.optimization_barrier((line_3[0], so_far))
        above_part, below_3 = lax.optimization_barrier((above_3[:, :projection], line_3[1]))
        block_4 = across(above_part, -1)
        pieces_4 = across(below_3[:, projection:], 1)
        line_3 = (above_3, below_3)
        so_far, pieces_3, last_rows = project(
            ring_at, near, far, line_3, (3, 5), projection, so_far
        )
        masks = (docs[:, None], docs[None, :], places[:, None], places[None, :])
        attended_far, held = far_attention(
            last_rows, so_far, block_4, masks, w_query.shape[1]
        )

    with jax.named_scope("output"):
        half = x_count * row_count
        pieces = (pieces, pieces_3, pieces_4)
        steps = early_steps + (3, 5, 4)
        theirs = output_half(half, True, ring_at, attended_far, pieces, steps)
        theirs, held = lax.optimization_barrier((theirs, held))
        received = shift(theirs, "core", 1)
        attended_near = near_attention(held, masks, w_query.shape[1])
        ours = output_half(half, False, ring_at, attended_near, pieces, steps)
        both = (ours.astype(jnp.float32) + received.astype(jnp.float32)).astype(jnp.bfloat16)
        parts = lax.all_to_all(both, "x", split_axis=0, concat_axis=0, tiled=True)
        return finish(parts.reshape(x_count, row_count, -1), turned)


def solution(mesh):
    grid = Mesh(mesh.devices.reshape(SIDE, SIDE, 4, 2), ("z", "y", "x", "core"))
    dp, tensor, rows = ("z", "y"), ("x", "core"), ("z", "y", "x", "core")
    return jax.shard_map(
        on_device,
        mesh=grid,
        in_specs=(
            P(rows, None),
            P(rows),
            P(rows),
            P(),
            P(dp, tensor),
            P(dp, tensor),
            P(dp, tensor),
            P(tensor, dp),
        ),
        out_specs=P(rows, None),
        check_vma=False,
    )
```
